32 devices in a mesh: src: 8 (over y, x, core), tm: 4 (over z).
Axes of the slice: x: 2, y: 2, z: 4, core: 2. Of those that a mesh axis runs over, the one named last changes fastest.
Arguments:
- attitude_design: float32 [4, 131072], P(None, ('src', 'tm')), may hold values from -6 to 6
- source_design: float32 [5, 131072], P(None, ('src', 'tm')), may hold values from -6 to 6
- scan_phase: float32 [131072], P(('src', 'tm')), may hold values from 0 to 1
- obs_weight: float32 [131072], P(('src', 'tm')), may hold values from 0.25 to 4
- obs_residual: float32 [131072], P(('src', 'tm')), may hold values from -6 to 6
- source_id: int32 [131072], P(('src', 'tm')), may hold values from 0 to 2047
- knot_start: int32 [131072], P(('src', 'tm')), may hold values from 0 to 1023
- time_segment: int32 [131072, 1], P(('src', 'tm')), may hold values from 0 to 3; in each aligned block of 4096 rows (0 to 4095, 4096 to 8191, ...) at most 2048 rows name the same one
Outputs:
- source_update: float32 [5, 16384], P(None, 'src')
- attitude_update: float32 [4, 4096], P(None, 'tm')
The draws below stay inside these ranges and needn't reach their ends.
Inputs may be any that keep to these rules, and one draw needn't show every extreme that they name: `time_segment`: among the observations of one device, at most 2048 fall in any one time segment, and in some device some segment receives exactly 2048.
All inputs are finite; a program needn't handle non-finite values.
Results may differ from the reference program's by a relative error of at most 0.0003.
Values sent between devices are 32-bit elements; how exact they have to be, the bound alone decides.
A program may use at most 64 MiB of HBM per device.

```python
import math
import jax
import jax.numpy as jnp
import numpy as np
from jax import lax

O_DEV = 4096
KS = 1024
S_DEV = 2048
ITERS = 4
NOBS = 131072
N_SRC = 8
N_TM = 4


def set_ends(values, key, least, high):
    extent = values.shape
    place = [jax.random.randint(jax.random.fold_in(key, axis), (), 0, extent[axis]) for axis in range(len(extent))]
    values = values.at[tuple(place)].set(least)
    longest = extent.index(max(extent))
    place[longest] = (place[longest] + 1) % extent[longest]
    return values.at[tuple(place)].set(high)


def block_levels(own_key, shape, cuts, low, top_value):
    def one(position, shards_of):
        heights = jax.random.uniform(jax.random.fold_in(jax.random.fold_in(own_key, 6), position), (shards_of,), jnp.float32, low / len(cuts), top_value / len(cuts))
        return jnp.repeat(jnp.exp(heights), shape[position] // shards_of).reshape((-1,) + (1,) * (len(shape) - position - 1))

    factor_of = one(*cuts[0])
    for cut in cuts[1:]:
        factor_of = factor_of * one(*cut)
    return factor_of


def shared_out(own_key, own, number, rows, amount, top, bound, slope):
    order = jax.random.permutation(own_key, amount)
    packed, common = portions_of(amount, rows * top, bound, slope, True), portions_of(amount, rows * top, bound, slope, False)
    places = jnp.arange(amount)

    def named(lengths, rotation):
        used = int((lengths > 0).sum())
        fixed = max(1, used // 4)
        passed = fixed + (places - fixed + rotation * (used - fixed)) % max(1, amount - fixed)
        return jnp.zeros((amount,), jnp.int32).at[order[jnp.where(places < fixed, places, passed)]].set(jnp.asarray(lengths, jnp.int32))

    lengths = jnp.where(number % 4 == 0, named(packed, number // 4), named(common, number - number // 4 - 1))
    mixed = jax.random.permutation(jax.random.fold_in(own, 3), amount)
    source_of, receiver = mixed[0:amount // 2 * 2:2], mixed[1:amount // 2 * 2:2]
    room = jnp.minimum(lengths[source_of] - 1, bound - lengths[receiver]) // 2
    room = jnp.where((source_of == order[0]) | (receiver == order[0]) | (lengths[receiver] == 0), 0, jnp.maximum(room, 0))
    passed = jax.random.randint(jax.random.fold_in(own, 4), (amount // 2,), 0, 1 << 20) % (room + 1)
    lengths = lengths.at[source_of].add(-passed).at[receiver].add(passed)
    items = jnp.searchsorted(jnp.cumsum(lengths), jnp.arange(rows * top), side="right").astype(jnp.int32)
    table = items.reshape(top, rows).T
    table = table[jax.random.permutation(jax.random.fold_in(own, 1), rows)]
    rotation = jax.random.randint(jax.random.fold_in(own, 2), (rows, 1), 0, top)
    return jnp.take_along_axis(table, (jnp.arange(top)[None, :] + rotation) % top, axis=1)


def portions_of(number_of, total, most, lean, full):
    weights = [(1 << 20) // math.isqrt(standing ** lean) + 1 for standing in range(1, number_of + 1)]
    largest = most if full else min(most, max(-(-total // number_of), total * weights[0] // sum(weights)))
    least = 1 if total - largest >= number_of - 1 else 0
    given, spare = [largest] + [least] * (number_of - 1), total - largest - least * (number_of - 1)
    while spare > 0:
        movable = [i for i in range(1, number_of) if given[i] < largest] or [i for i in range(1, number_of) if given[i] < most]
        mass, budget = sum([weights[i] for i in movable]), spare
        for i in movable:
            addition = min(most - given[i], max(1, budget * weights[i] // mass), spare)
            given[i] = given[i] + addition
            spare = spare - addition
    return np.array(given)


def bell_draw(stream_key, extent, scale, reach, cuts=(), held_as=jnp.bfloat16):
    values = jax.random.normal(stream_key, extent, jnp.float32) * scale
    if len(cuts) > 0:
        values = block_levels(stream_key, extent, cuts, -0.22, 0.18) * values
    return jnp.clip(values, min=-reach, max=reach).astype(held_as)


def setup_inputs(seed: int = 0) -> dict:
    keys = jax.random.split(jax.random.key(seed), 9)
    attitude_design = bell_draw(keys[0], (4, NOBS), 1.0, 6.0, ((1, 32),), jnp.float32)
    source_design = bell_draw(keys[1], (5, NOBS), 1.0, 6.0, ((1, 32),), jnp.float32)
    scan_phase = jnp.clip(1.0 * jax.random.uniform(keys[2], (NOBS,), jnp.float32) ** block_levels(keys[2], (NOBS,), ((0, 32),), -0.2, 0.2), 0.0, 1.0)
    obs_weight = jnp.clip(jnp.exp(math.log(4.0) - 2.7725887 * jax.random.uniform(keys[3], (NOBS,), jnp.float32) ** block_levels(keys[3], (NOBS,), ((0, 32),), -0.2, 0.2)), 0.25, 4.0)
    obs_residual = bell_draw(keys[4], (NOBS,), 1.0, 6.0, ((0, 32),), jnp.float32)
    source_id = set_ends(jax.random.randint(keys[5], (NOBS,), 0, S_DEV), jax.random.fold_in(keys[5], 1), 0, S_DEV - 1).astype(jnp.int32)
    knot_start = set_ends(jax.random.randint(keys[6], (NOBS,), 0, KS), jax.random.fold_in(keys[6], 1), 0, KS - 1).astype(jnp.int32)
    time_segment_keys = jax.random.split(jax.random.fold_in(keys[7], 1), NOBS // O_DEV)
    time_segment_turns = jax.random.permutation(jax.random.fold_in(keys[7], 3), NOBS // O_DEV)
    time_segment = jax.vmap(lambda own, number: shared_out(jax.random.fold_in(keys[7], 2), own, number, O_DEV, N_TM, 1, 2 * O_DEV // N_TM, 2))(time_segment_keys, time_segment_turns).reshape((NOBS, 1))
    return {"attitude_design": attitude_design, "source_design": source_design, "scan_phase": scan_phase, "obs_weight": obs_weight, "obs_residual": obs_residual, "source_id": source_id, "knot_start": knot_start, "time_segment": time_segment}


prior_source = 1.0
prior_attitude = 1.0
index_pairs = [(i, j) for i in range(5) for j in range(i, 5)]

def spline_weights(fraction):
    rest = 1.0 - fraction
    square = fraction * fraction
    cube = square * fraction
    return [rest * rest * rest / 6.0, (3.0 * cube - 6.0 * square + 4.0) / 6.0, (-3.0 * cube + 3.0 * square + 3.0 * fraction + 1.0) / 6.0, cube / 6.0]

def band_values(attitude, fraction, weights, reduced):
    basis = spline_weights(fraction)
    outer = (attitude[:, None, :] * attitude[None, :, :]).reshape(16, -1)
    zero_rows = jnp.zeros_like(outer)
    stacked = []
    for j in range(4):
        pieces = []
        for d in range(4):
            if j + d <= 3:
                pieces.append(outer * (weights * basis[j] * basis[j + d])[None, :])
            else:
                pieces.append(zero_rows)
        pieces.append(attitude * (weights * basis[j] * reduced)[None, :])
        stacked.append(jnp.concatenate(pieces, 0))
    values = jnp.stack(stacked, 0)
    return jnp.transpose(values, (0, 2, 1)).reshape(-1, 68)

def band_index(first):
    return (first[None, :] + jnp.arange(4, dtype=jnp.int32)[:, None]).reshape(-1).astype(jnp.int32)

def source_values(design, weights, resid):
    pieces = [weights * design[i] * design[j] for i, j in index_pairs]
    pieces = pieces + [weights * design[i] * resid for i in range(5)]
    return jnp.stack(pieces, 1)

def solve_five(normals):
    entry = {}
    for n, (i, j) in enumerate(index_pairs):
        entry[j, i] = normals[n]
    for i in range(5):
        entry[i, i] = entry[i, i] + prior_source
    lower = {}
    for i in range(5):
        for j in range(i + 1):
            value = entry[i, j]
            for k in range(j):
                value = value - lower[i, k] * lower[j, k]
            if i == j:
                lower[i, i] = jnp.sqrt(value)
            else:
                lower[i, j] = value / lower[j, j]
    forward = []
    for i in range(5):
        value = normals[15 + i]
        for k in range(i):
            value = value - lower[i, k] * forward[k]
        forward.append(value / lower[i, i])
    solution = [None] * 5
    for i in range(4, -1, -1):
        value = forward[i]
        for k in range(i + 1, 5):
            value = value - lower[k, i] * solution[k]
        solution[i] = value / lower[i, i]
    return jnp.stack(solution, 0)

def apply_band(matrix, matrix_ext, padded, columns):
    result = prior_attitude * padded[:, 3:3 + columns]
    for d in range(4):
        block_mat = matrix[16 * d:16 * d + 16].reshape(4, 4, columns)
        result = result + jnp.einsum('abk,bk->ak', block_mat, padded[:, 3 + d:3 + d + columns], precision=lax.Precision.HIGHEST)
    for d in range(1, 4):
        block_mat = matrix_ext[16 * d:16 * d + 16, 3 - d:3 - d + columns].reshape(4, 4, columns)
        result = result + jnp.einsum('bak,bk->ak', block_mat, padded[:, 3 - d:3 - d + columns], precision=lax.Precision.HIGHEST)
    return result

def reference(attitude_design, source_design, scan_phase, obs_weight, obs_residual, source_id, knot_start, time_segment):
    n_obs = scan_phase.shape[0]
    device_block = jnp.arange(n_obs, dtype=jnp.int32) // O_DEV
    global_source = device_block // N_TM * S_DEV + source_id
    contrib = source_values(source_design, obs_weight, obs_residual)
    normals = jax.ops.segment_sum(contrib, global_source, num_segments=S_DEV * N_SRC).T
    source_update = solve_five(normals)
    picked = source_update[:, global_source]
    reduced = obs_residual - lax.optimization_barrier(jnp.sum(source_design * picked, axis=0))
    knot_count = KS * N_TM
    first = (time_segment[:, 0] * KS + knot_start).astype(jnp.int32)
    nblocks = n_obs // O_DEV
    att_blocks = jnp.transpose(attitude_design.reshape(4, nblocks, O_DEV), (1, 0, 2))

    def add_block(summed, pieces):
        att, frac, wts, res, start = pieces
        values = band_values(att, frac, wts, res)
        return (summed + jax.ops.segment_sum(values, band_index(start), num_segments=knot_count + 3), None)
    start_acc = jnp.zeros((knot_count + 3, 68), jnp.float32)
    summed, _ = lax.scan(add_block, start_acc, (att_blocks, scan_phase.reshape(nblocks, O_DEV), obs_weight.reshape(nblocks, O_DEV), reduced.reshape(nblocks, O_DEV), first.reshape(nblocks, O_DEV)))
    band = summed[:knot_count].T
    matrix = band[:64]
    matrix_ext = jnp.pad(matrix, ((0, 0), (3, 0)))
    rhs = band[64:68]

    def image_of(field):
        return apply_band(matrix, matrix_ext, jnp.pad(field, ((0, 0), (3, 3))), knot_count)
    solution = jnp.zeros_like(rhs)
    resid = rhs
    direction = rhs
    norm_now = jnp.sum(resid * resid)
    for step in range(ITERS):
        image = image_of(direction)
        alpha = norm_now / jnp.sum(direction * image)
        solution = solution + alpha * direction
        resid = resid - alpha * image
        norm_next = jnp.sum(resid * resid)
        direction = resid + norm_next / norm_now * direction
        norm_now = norm_next
    return (source_update, solution)
```

```python
import functools

import jax
import jax.numpy as jnp
from jax import lax
from jax.experimental import pallas as pl
from jax.experimental.pallas import tpu as pltpu
from jax.sharding import PartitionSpec as P

KS = 1024
S_DEV = 2048
ITERS = 4
ROWS = 48
SRC_GROUPS = 8
SRC_WIDE = S_DEV // SRC_GROUPS
MESH = pl.DeviceIdType.MESH

prior_source = 1.0
prior_attitude = 1.0
index_pairs = [(i, j) for i in range(5) for j in range(i, 5)]
component_pairs = [(c, e) for c in range(4) for e in range(c, 4)]
NT = (((1,), (1,)), ((), ()))


def split(x):
    high = x.astype(jnp.bfloat16)
    low = (x - high.astype(jnp.float32)).astype(jnp.bfloat16)
    return high, low


def onehot(count, index, base):
    place = lax.broadcasted_iota(jnp.int32, (count, index.shape[1]), 0) + base
    return jnp.where(place == index, 1.0, 0.0).astype(jnp.bfloat16)


def source_kernel(design_ref, weight_ref, resid_ref, id_ref, out_ref, lhs):
    q = [design_ref[i : i + 1, :] for i in range(5)]
    w = weight_ref[...]
    r = resid_ref[...]
    wq = [w * q[i] for i in range(5)]
    rows = [wq[i] * q[j] for i, j in index_pairs] + [wq[i] * r for i in range(5)]
    rows += [jnp.zeros_like(w)] * 4
    high, low = split(jnp.concatenate(rows, 0))
    both = jnp.concatenate([high.astype(jnp.float32), low.astype(jnp.float32)], 0)
    ids = id_ref[...]
    group = ids // SRC_WIDE
    for a in range(SRC_GROUPS):
        lhs[48 * a : 48 * a + 48, :] = jnp.where(group == a, both, 0.0).astype(jnp.bfloat16)
    hot = onehot(SRC_WIDE, ids % SRC_WIDE, 0)
    got = lax.dot_general(lhs[...], hot, NT, preferred_element_type=jnp.float32)
    for a in range(SRC_GROUPS):
        out_ref[a] = got[48 * a : 48 * a + 24] + got[48 * a + 24 : 48 * a + 48]


def solve_five(normals):
    entry = {}
    for n, (i, j) in enumerate(index_pairs):
        entry[j, i] = normals[n]
    for i in range(5):
        entry[i, i] = entry[i, i] + prior_source
    lower = {}
    for i in range(5):
        for j in range(i + 1):
            value = entry[i, j]
            for k in range(j):
                value = value - lower[i, k] * lower[j, k]
            if i == j:
                lower[i, i] = jnp.sqrt(value)
            else:
                lower[i, j] = value / lower[j, j]
    forward = []
    for i in range(5):
        value = normals[15 + i]
        for k in range(i):
            value = value - lower[i, k] * forward[k]
        forward.append(value / lower[i, i])
    result = [None] * 5
    for i in range(4, -1, -1):
        value = forward[i]
        for k in range(i + 1, 5):
            value = value - lower[k, i] * result[k]
        result[i] = value / lower[i, i]
    return result


def greet(peers):
    barrier = pltpu.get_barrier_semaphore()
    for peer in peers:
        pl.semaphore_signal(barrier, inc=1, device_id=peer, device_id_type=MESH)
    pl.semaphore_wait(barrier, len(peers))


def send(src, dst, sems, slot, peer):
    copy = pltpu.make_async_remote_copy(
        src_ref=src,
        dst_ref=dst,
        send_sem=sems.at[0, slot],
        recv_sem=sems.at[1, slot],
        device_id=peer,
        device_id_type=MESH,
    )
    copy.start()
    return copy


def normals_kernel(n_tm, own_ref, full_ref, update_ref, landed, gathered, sem_a, sem_b):
    me_s, me_t = lax.axis_index("src"), lax.axis_index("tm")
    part = SRC_GROUPS // n_tm
    at = [(me_s, lax.rem(me_t + o, n_tm)) for o in range(1, n_tm)]
    greet(at)
    copies = []
    for o in range(1, n_tm):
        copies.append(
            send(own_ref.at[pl.ds(at[o - 1][1] * part, part)], landed.at[o - 1], sem_a, o - 1, at[o - 1])
        )
    total = own_ref[pl.ds(me_t * part, part)]
    for o in range(1, n_tm):
        copies[o - 1].wait_recv()
        total = total + landed[o - 1]
    solved = solve_five([total[:, n, :] for n in range(20)])
    mine = pl.ds(me_t * part, part)
    for i in range(5):
        for g in range(part):
            gathered[me_t * part + g, i : i + 1, :] = solved[i][g : g + 1, :]
    for g in range(part):
        gathered[me_t * part + g, 5:8, :] = jnp.zeros((3, SRC_WIDE), jnp.float32)
    more = []
    for o in range(1, n_tm):
        more.append(send(gathered.at[mine], gathered.at[mine], sem_b, o - 1, at[o - 1]))
    for copy in copies:
        copy.wait_send()
    for copy in more:
        copy.wait()
    for a in range(SRC_GROUPS):
        block = gathered[a]
        full_ref[a] = block
        update_ref[:, a * SRC_WIDE : (a + 1) * SRC_WIDE] = block[0:5]


def knot_kernel(
    n_seg,
    full_ref,
    attitude_ref,
    design_ref,
    phase_ref,
    weight_ref,
    resid_ref,
    id_ref,
    start_ref,
    segment_ref,
    out_ref,
    feat,
    lhs,
    acc,
):
    n_obs = phase_ref.shape[1]
    ids = id_ref[...]
    group = ids // SRC_WIDE
    hot = onehot(SRC_WIDE, ids % SRC_WIDE, 0)
    table = full_ref[...].reshape(SRC_GROUPS * 8, SRC_WIDE)
    high, low = split(table)
    picks = jnp.dot(high, hot, preferred_element_type=jnp.float32) + jnp.dot(
        low, hot, preferred_element_type=jnp.float32
    )
    picked = jnp.zeros((8, n_obs), jnp.float32)
    for a in range(SRC_GROUPS):
        picked = picked + jnp.where(group == a, picks[8 * a : 8 * a + 8], 0.0)
    fitted = jnp.sum(design_ref[...] * picked[0:5], axis=0, keepdims=True)
    reduced = resid_ref[...] - fitted

    t = phase_ref[...]
    w = weight_ref[...]
    rest = 1.0 - t
    square = t * t
    cube = square * t
    basis = [
        rest * rest * rest / 6.0,
        (3.0 * cube - 6.0 * square + 4.0) / 6.0,
        (-3.0 * cube + 3.0 * square + 3.0 * t + 1.0) / 6.0,
        cube / 6.0,
    ]
    att = attitude_ref[...]
    outer = jnp.concatenate([att[c : c + 1] * att[e : e + 1] for c, e in component_pairs], 0)
    top = 0
    for j in range(4):
        scaled = w * basis[j]
        pieces = [att * (scaled * reduced)]
        for d in range(4 - j):
            pieces.append(outer * (scaled * basis[j + d]))
        size = 44 - 10 * j
        room = (48, 40, 24, 16)[j]
        if room > size:
            pieces.append(jnp.zeros((room - size, n_obs), jnp.float32))
        block_high, block_low = split(jnp.concatenate(pieces, 0))
        feat[top : top + room, :] = block_high.astype(jnp.float32)
        feat[128 + top : 128 + top + room, :] = block_low.astype(jnp.float32)
        top += room

    segment = segment_ref[...]
    for s in range(n_seg):
        lhs[256 * s : 256 * s + 256, :] = jnp.where(segment == s, feat[...], 0.0).astype(
            jnp.bfloat16
        )
    start = start_ref[...]

    def tile(n, carry):
        knots = onehot(256, start, n * 256)
        place = pl.ds(pl.multiple_of(n * 256, 256), 256)
        acc[:, place] = lax.dot_general(lhs[...], knots, NT, preferred_element_type=jnp.float32)
        return carry

    lax.fori_loop(0, KS // 256, tile, 0)

    lane = lax.broadcasted_iota(jnp.int32, (1, KS), 1)
    before = [None] * 4
    for s in range(n_seg):
        total = None
        top = 0
        for j in range(4):
            room = (48, 40, 24, 16)[j]
            base = 256 * s + top
            value = acc[base : base + room, :] + acc[base + 128 : base + 128 + room, :]
            top += room
            if j == 0:
                total = value
                continue
            size = 44 - 10 * j
            value = pltpu.roll(value, j, 1)
            carried = 0.0 if before[j] is None else before[j]
            before[j] = value
            value = jnp.where(lane < j, carried, value)
            if room > size:
                value = jnp.where(lax.broadcasted_iota(jnp.int32, (room, 1), 0) < size, value, 0.0)
            total = total + jnp.concatenate([value, jnp.zeros((48 - room, KS), jnp.float32)], 0) if room < 48 else total + value
        out_ref[s] = total.reshape(ROWS, 8, 128)


def shifted(x, by):
    lane = lax.broadcasted_iota(jnp.int32, x.shape, 2)
    turned = pltpu.roll(x, (128 - by) % 128, 2)
    if by > 0:
        return jnp.where(lane >= 128 - by, pltpu.roll(turned, 15, 1), turned)
    return jnp.where(lane < -by, pltpu.roll(turned, 1, 1), turned)


def attitude_kernel(
    n_src, n_tm, part_ref, out_ref, rs1, s1, rs2, full, stage, halo, ext, red, red_in,
    sem_a, sem_b, sem_c, sem_d, sem_e,
):
    me_s, me_t = lax.axis_index("src"), lax.axis_index("tm")
    rows = ROWS // n_src
    side = [(lax.rem(me_s + o, n_src), me_t) for o in range(1, n_src)]
    line = [(me_s, lax.rem(me_t + o, n_tm)) for o in range(1, n_tm)]
    greet(side + line)

    copies = []
    for o in range(1, n_src):
        peer = side[o - 1]
        copies.append(
            send(part_ref.at[:, pl.ds(peer[0] * rows, rows)], rs1.at[o - 1], sem_a, o - 1, peer)
        )
    total = part_ref[:, pl.ds(me_s * rows, rows)]
    for o in range(1, n_src):
        copies[o - 1].wait_recv()
        total = total + rs1[o - 1]
    s1[...] = total
    second = []
    for o in range(1, n_tm):
        peer = line[o - 1]
        second.append(send(s1.at[peer[1]], rs2.at[o - 1], sem_b, o - 1, peer))
    total = s1[me_t]
    for o in range(1, n_tm):
        second[o - 1].wait_recv()
        total = total + rs2[o - 1]
    mine = pl.ds(me_s * rows, rows)
    full[mine] = total
    third = []
    for o in range(1, n_src):
        third.append(send(full.at[mine], full.at[mine], sem_c, o - 1, side[o - 1]))
    for copy in copies + second:
        copy.wait_send()
    for copy in third:
        copy.wait()

    whole = full[...]
    stage[0] = whole[:, 0, :]
    stage[1] = whole[:, 7, :]
    ahead, behind = line[0], line[n_tm - 2]
    to_behind = send(stage.at[0], halo.at[0], sem_d, 0, behind)
    to_ahead = send(stage.at[1], halo.at[1], sem_d, 1, ahead)
    ext[:, 0:8, :] = whole
    ext[:, 8:16, :] = jnp.zeros((ROWS, 8, 128), jnp.float32)
    to_behind.wait()
    to_ahead.wait()
    ext[:, 8, :] = halo[0] * jnp.where(me_t < n_tm - 1, 1.0, 0.0)
    ext[:, 15, :] = halo[1] * jnp.where(me_t > 0, 1.0, 0.0)

    row = lax.broadcasted_iota(jnp.int32, (1, 16, 128), 1)
    kept = jnp.where(row < 8, 1.0, 0.0)
    kept = kept + jnp.where(row == 8, 1.0, 0.0) * jnp.where(me_t < n_tm - 1, 1.0, 0.0)
    kept = kept + jnp.where(row == 15, 1.0, 0.0) * jnp.where(me_t > 0, 1.0, 0.0)
    columns = []
    for d in range(4):
        for e in range(4):
            columns.append(
                jnp.stack(
                    [
                        ext[4 + 10 * d + component_pairs.index((min(c, e), max(c, e)))]
                        for c in range(4)
                    ],
                    0,
                )
            )

    def multiply(d, x):
        value = columns[4 * d] * x[0:1]
        for e in range(1, 4):
            value = value + columns[4 * d + e] * x[e : e + 1]
        return value

    def image_of(x):
        value = prior_attitude * x + multiply(0, x)
        for d in range(1, 4):
            value = value + multiply(d, shifted(x, d)) + shifted(multiply(d, x), -d)
        return value * kept

    resid = ext[0:4]
    direction = resid
    field = None
    image = None
    alpha = None
    gamma_old = None
    for step in range(ITERS):
        applied = image_of(resid)
        inner = resid[:, 0:8, :]
        red[step, 0] = jnp.sum(inner * inner, axis=0)
        red[step, 1] = jnp.sum(inner * applied[:, 0:8, :], axis=0)
        sums = []
        for o in range(1, n_tm):
            sums.append(
                send(red.at[step], red_in.at[step, o - 1], sem_e, step * (n_tm - 1) + o - 1, line[o - 1])
            )
        value = red[step]
        for o in range(1, n_tm):
            sums[o - 1].wait()
            value = value + red_in[step, o - 1]
        gamma = jnp.sum(value[0:1], axis=(1, 2), keepdims=True)
        delta = jnp.sum(value[1:2], axis=(1, 2), keepdims=True)
        if step == 0:
            alpha = gamma / delta
            direction, image = resid, applied
            field = alpha * direction
        else:
            beta = gamma / gamma_old
            alpha = gamma / (delta - beta * (gamma / alpha))
            direction = resid + beta * direction
            image = applied + beta * image
            field = field + alpha * direction
        resid = resid - alpha * image
        gamma_old = gamma
    out_ref[...] = field[:, 0:8, :]


def vmem(count):
    return [pl.BlockSpec(memory_space=pltpu.VMEM)] * count


def body(
    n_src,
    n_tm,
    attitude_design,
    source_design,
    scan_phase,
    obs_weight,
    obs_residual,
    source_id,
    knot_start,
    time_segment,
):
    n_obs = scan_phase.shape[0]
    f32 = jnp.float32
    flat = lambda x: x.reshape(1, n_obs)
    phase, weight, resid = flat(scan_phase), flat(obs_weight), flat(obs_residual)
    ids, start, segment = flat(source_id), flat(knot_start), flat(time_segment)
    limit = pltpu.CompilerParams(vmem_limit_bytes=56 * 1024 * 1024)
    own = pl.pallas_call(
        source_kernel,
        out_shape=jax.ShapeDtypeStruct((SRC_GROUPS, 24, SRC_WIDE), f32),
        in_specs=vmem(4),
        out_specs=vmem(1)[0],
        scratch_shapes=[pltpu.VMEM((48 * SRC_GROUPS, n_obs), jnp.bfloat16)],
        compiler_params=limit,
    )(source_design, weight, resid, ids)
    part = SRC_GROUPS // n_tm
    full, update = pl.pallas_call(
        functools.partial(normals_kernel, n_tm),
        out_shape=[
            jax.ShapeDtypeStruct((SRC_GROUPS, 8, SRC_WIDE), f32),
            jax.ShapeDtypeStruct((5, S_DEV), f32),
        ],
        in_specs=vmem(1),
        out_specs=vmem(2),
        scratch_shapes=[
            pltpu.VMEM((n_tm - 1, part, 24, SRC_WIDE), f32),
            pltpu.VMEM((SRC_GROUPS, 8, SRC_WIDE), f32),
            pltpu.SemaphoreType.DMA((2, n_tm - 1)),
            pltpu.SemaphoreType.DMA((2, n_tm - 1)),
        ],
        compiler_params=pltpu.CompilerParams(collective_id=0, has_side_effects=True),
    )(own)
    partial_band = pl.pallas_call(
        functools.partial(knot_kernel, n_tm),
        out_shape=jax.ShapeDtypeStruct((n_tm, ROWS, 8, 128), f32),
        in_specs=vmem(9),
        out_specs=vmem(1)[0],
        scratch_shapes=[
            pltpu.VMEM((256, n_obs), f32),
            pltpu.VMEM((256 * n_tm, n_obs), jnp.bfloat16),
            pltpu.VMEM((256 * n_tm, KS), f32),
        ],
        compiler_params=limit,
    )(full, attitude_design, source_design, phase, weight, resid, ids, start, segment)
    rows = ROWS // n_src
    field = pl.pallas_call(
        functools.partial(attitude_kernel, n_src, n_tm),
        out_shape=jax.ShapeDtypeStruct((4, 8, 128), f32),
        in_specs=vmem(1),
        out_specs=vmem(1)[0],
        scratch_shapes=[
            pltpu.VMEM((n_src - 1, n_tm, rows, 8, 128), f32),
            pltpu.VMEM((n_tm, rows, 8, 128), f32),
            pltpu.VMEM((n_tm - 1, rows, 8, 128), f32),
            pltpu.VMEM((ROWS, 8, 128), f32),
            pltpu.VMEM((2, ROWS, 128), f32),
            pltpu.VMEM((2, ROWS, 128), f32),
            pltpu.VMEM((ROWS, 16, 128), f32),
            pltpu.VMEM((ITERS, 2, 8, 128), f32),
            pltpu.VMEM((ITERS, n_tm - 1, 2, 8, 128), f32),
            pltpu.SemaphoreType.DMA((2, n_src - 1)),
            pltpu.SemaphoreType.DMA((2, n_tm - 1)),
            pltpu.SemaphoreType.DMA((2, n_src - 1)),
            pltpu.SemaphoreType.DMA((2, 2)),
            pltpu.SemaphoreType.DMA((2, ITERS * (n_tm - 1))),
        ],
        compiler_params=pltpu.CompilerParams(
            collective_id=1, has_side_effects=True, vmem_limit_bytes=56 * 1024 * 1024
        ),
    )(partial_band)
    return update, field.reshape(4, KS)


def solution(mesh):
    n_src, n_tm = mesh.shape["src"], mesh.shape["tm"]
    both = ("src", "tm")
    in_specs = (
        P(None, both),
        P(None, both),
        P(both),
        P(both),
        P(both),
        P(both),
        P(both),
        P(both, None),
    )
    out_specs = (P(None, "src"), P(None, "tm"))
    return jax.shard_map(
        functools.partial(body, n_src, n_tm),
        mesh=mesh,
        in_specs=in_specs,
        out_specs=out_specs,
        check_vma=False,
    )
```

```python
import functools

import jax
import jax.numpy as jnp
from jax import lax
from jax.experimental import pallas as pl
from jax.experimental.pallas import tpu as pltpu
from jax.sharding import PartitionSpec as P

KS = 1024
S_DEV = 2048
ITERS = 4
ROOMS = (40, 32, 24, 16)
FEATS = sum(ROOMS)
SRC_GROUPS = 8
SRC_WIDE = S_DEV // SRC_GROUPS
MESH = pl.DeviceIdType.MESH

prior_source = 1.0
prior_attitude = 1.0
index_pairs = [(i, j) for i in range(5) for j in range(i, 5)]
component_pairs = [(c, e) for c in range(4) for e in range(c, 4)]
NT = (((1,), (1,)), ((), ()))


def split(x):
    high = x.astype(jnp.bfloat16)
    low = (x - high.astype(jnp.float32)).astype(jnp.bfloat16)
    return high, low


def onehot(count, index, base):
    place = lax.broadcasted_iota(jnp.int32, (count, index.shape[1]), 0) + base
    return jnp.where(place == index, 1.0, 0.0).astype(jnp.bfloat16)


def solve_five(normals):
    entry = {}
    for n, (i, j) in enumerate(index_pairs):
        entry[j, i] = normals[n]
    for i in range(5):
        entry[i, i] = entry[i, i] + prior_source
    lower = {}
    for i in range(5):
        for j in range(i + 1):
            value = entry[i, j]
            for k in range(j):
                value = value - lower[i, k] * lower[j, k]
            if i == j:
                lower[i, i] = jnp.sqrt(value)
            else:
                lower[i, j] = value / lower[j, j]
    forward = []
    for i in range(5):
        value = normals[15 + i]
        for k in range(i):
            value = value - lower[i, k] * forward[k]
        forward.append(value / lower[i, i])
    result = [None] * 5
    for i in range(4, -1, -1):
        value = forward[i]
        for k in range(i + 1, 5):
            value = value - lower[k, i] * result[k]
        result[i] = value / lower[i, i]
    return result


def send(src, dst, sems, slot, peer):
    copy = pltpu.make_async_remote_copy(
        src_ref=src,
        dst_ref=dst,
        send_sem=sems.at[0, slot],
        recv_sem=sems.at[1, slot],
        device_id=peer,
        device_id_type=MESH,
    )
    copy.start()
    return copy


def shifted(x, by):
    lane = lax.broadcasted_iota(jnp.int32, x.shape, 2)
    turned = pltpu.roll(x, (128 - by) % 128, 2)
    if by > 0:
        return jnp.where(lane >= 128 - by, pltpu.roll(turned, 15, 1), turned)
    return jnp.where(lane < -by, pltpu.roll(turned, 1, 1), turned)


def source_sums(design, w, r, ids, lhs, own_ref):
    q = [design[i : i + 1, :] for i in range(5)]
    wq = [w * q[i] for i in range(5)]
    rows = [wq[i] * q[j] for i, j in index_pairs] + [wq[i] * r for i in range(5)]
    rows += [jnp.zeros_like(w)] * 4
    high, low = split(jnp.concatenate(rows, 0))
    both = jnp.concatenate([high.astype(jnp.float32), low.astype(jnp.float32)], 0)
    group = ids // SRC_WIDE
    for a in range(SRC_GROUPS):
        lhs[48 * a : 48 * a + 48, :] = jnp.where(group == a, both, 0.0).astype(jnp.bfloat16)
    hot = onehot(SRC_WIDE, ids % SRC_WIDE, 0)
    got = lax.dot_general(lhs[...], hot, NT, preferred_element_type=jnp.float32)
    for a in range(SRC_GROUPS):
        own_ref[a] = got[48 * a : 48 * a + 24] + got[48 * a + 24 : 48 * a + 48]


def behind(value, by, carried, lane):
    value = pltpu.roll(value, by, 1)
    front = 0.0 if carried is None else carried
    return value, jnp.where(lane < by, front, value)


def kernel(
    n_src, n_tm,
    attitude_ref, design_ref, phase_ref, weight_ref, resid_ref, id_ref, start_ref, segment_ref,
    update_ref, out_ref,
    own, landed, gathered, lhs_s, feat, lhs, acc, feat_r, lhs_r, acc_r,
    part, part_r, rs1, s1, rs2, full, rhs_in, rhs_all,
    stage, halo, ext, red, red_in,
    sem_n, sem_g, sem_a, sem_b, sem_c, sem_p, sem_q, sem_d, sem_e,
):
    me_s, me_t = lax.axis_index("src"), lax.axis_index("tm")
    n_obs = phase_ref.shape[1]
    side = [(lax.rem(me_s + o, n_src), me_t) for o in range(1, n_src)]
    line = [(me_s, lax.rem(me_t + o, n_tm)) for o in range(1, n_tm)]
    barrier = pltpu.get_barrier_semaphore()
    for peer in side + line:
        pl.semaphore_signal(barrier, inc=1, device_id=peer, device_id_type=MESH)

    w, ids = weight_ref[...], id_ref[...]
    source_sums(design_ref, w, resid_ref[...], ids, lhs_s, own)
    pl.semaphore_wait(barrier, len(side) + len(line))
    part_s = SRC_GROUPS // n_tm
    normals = []
    for o in range(1, n_tm):
        peer = line[o - 1]
        normals.append(
            send(own.at[pl.ds(peer[1] * part_s, part_s)], landed.at[o - 1], sem_n, o - 1, peer)
        )

    t = phase_ref[...]
    rest = 1.0 - t
    square = t * t
    cube = square * t
    basis = [
        rest * rest * rest / 6.0,
        (3.0 * cube - 6.0 * square + 4.0) / 6.0,
        (-3.0 * cube + 3.0 * square + 3.0 * t + 1.0) / 6.0,
        cube / 6.0,
    ]
    att = attitude_ref[...]
    outer = jnp.concatenate([att[c : c + 1] * att[e : e + 1] for c, e in component_pairs], 0)
    top = 0
    for j in range(4):
        scaled = w * basis[j]
        pieces = [outer * (scaled * basis[j + d]) for d in range(4 - j)]
        if ROOMS[j] > 40 - 10 * j:
            pieces.append(jnp.zeros((ROOMS[j] - 40 + 10 * j, n_obs), jnp.float32))
        high, low = split(jnp.concatenate(pieces, 0))
        feat[top : top + ROOMS[j], :] = high.astype(jnp.float32)
        feat[FEATS + top : FEATS + top + ROOMS[j], :] = low.astype(jnp.float32)
        top += ROOMS[j]
    segment, start = segment_ref[...], start_ref[...]
    tall = 2 * FEATS
    for s in range(n_tm):
        lhs[tall * s : tall * s + tall, :] = jnp.where(segment == s, feat[...], 0.0).astype(
            jnp.bfloat16
        )

    def tile(n, carry):
        knots = onehot(256, start, n * 256)
        place = pl.ds(pl.multiple_of(n * 256, 256), 256)
        acc[:, place] = lax.dot_general(lhs[...], knots, NT, preferred_element_type=jnp.float32)
        return carry

    tiles = KS // 256
    lax.fori_loop(0, tiles // 2, tile, 0)

    mine = pl.ds(me_t * part_s, part_s)
    total = own[mine]
    for o in range(1, n_tm):
        normals[o - 1].wait_recv()
        total = total + landed[o - 1]
    solved = solve_five([total[:, n, :] for n in range(20)])
    for g in range(part_s):
        for i in range(5):
            gathered[me_t * part_s + g, i : i + 1, :] = solved[i][g : g + 1, :]
        gathered[me_t * part_s + g, 5:8, :] = jnp.zeros((3, SRC_WIDE), jnp.float32)
    gathers = []
    for o in range(1, n_tm):
        gathers.append(send(gathered.at[mine], gathered.at[mine], sem_g, o - 1, line[o - 1]))

    lax.fori_loop(tiles // 2, tiles, tile, 0)

    lane = lax.broadcasted_iota(jnp.int32, (1, KS), 1)
    rows_all = part.shape[1]
    before = [None] * 4
    for s in range(n_tm):
        total = None
        top = tall * s
        for j in range(4):
            room, size = ROOMS[j], 40 - 10 * j
            value = acc[top : top + room, :] + acc[FEATS + top : FEATS + top + room, :]
            top += room
            if j == 0:
                total = value
                continue
            before[j], value = behind(value, j, before[j], lane)
            total = total + jnp.concatenate([value, jnp.zeros((40 - room, KS), jnp.float32)], 0)
        part[s, 0:40] = total.reshape(40, 8, 128)
        if rows_all > 40:
            part[s, 40:rows_all] = jnp.zeros((rows_all - 40, 8, 128), jnp.float32)
    rows = rows_all // n_src
    first = []
    for o in range(1, n_src):
        peer = side[o - 1]
        first.append(
            send(part.at[:, pl.ds(peer[0] * rows, rows)], rs1.at[o - 1], sem_a, o - 1, peer)
        )

    for copy in gathers:
        copy.wait()
    for copy in normals:
        copy.wait_send()
    for a in range(SRC_GROUPS):
        update_ref[:, a * SRC_WIDE : (a + 1) * SRC_WIDE] = gathered[a, 0:5]
    group = ids // SRC_WIDE
    hot = onehot(SRC_WIDE, ids % SRC_WIDE, 0)
    high, low = split(gathered[...].reshape(SRC_GROUPS * 8, SRC_WIDE))
    picks = jnp.dot(high, hot, preferred_element_type=jnp.float32) + jnp.dot(
        low, hot, preferred_element_type=jnp.float32
    )
    picked = jnp.zeros((8, n_obs), jnp.float32)
    for a in range(SRC_GROUPS):
        picked = picked + jnp.where(group == a, picks[8 * a : 8 * a + 8], 0.0)
    fitted = jnp.sum(design_ref[...] * picked[0:5], axis=0, keepdims=True)
    weighted = w * (resid_ref[...] - fitted)
    high, low = split(jnp.concatenate([att * (weighted * basis[j]) for j in range(4)], 0))
    feat_r[0:16, :] = high.astype(jnp.float32)
    feat_r[16:32, :] = low.astype(jnp.float32)
    for s in range(n_tm):
        lhs_r[32 * s : 32 * s + 32, :] = jnp.where(segment == s, feat_r[...], 0.0).astype(
            jnp.bfloat16
        )

    def tile_r(n, carry):
        knots = onehot(256, start, n * 256)
        place = pl.ds(pl.multiple_of(n * 256, 256), 256)
        acc_r[:, place] = lax.dot_general(lhs_r[...], knots, NT, preferred_element_type=jnp.float32)
        return carry

    lax.fori_loop(0, tiles, tile_r, 0)
    before = [None] * 4
    for s in range(n_tm):
        total = None
        for j in range(4):
            top = 32 * s + 4 * j
            value = acc_r[top : top + 4, :] + acc_r[16 + top : 20 + top, :]
            if j == 0:
                total = value
                continue
            before[j], value = behind(value, j, before[j], lane)
            total = total + value
        part_r[s] = total.reshape(4, 8, 128)

    rhs_first = []
    for o in range(1, n_tm):
        peer = line[o - 1]
        rhs_first.append(send(part_r.at[peer[1]], rhs_in.at[o - 1], sem_p, o - 1, peer))
    own_rows = pl.ds(me_s * rows, rows)
    total = part[:, own_rows]
    for o in range(1, n_src):
        first[o - 1].wait_recv()
        total = total + rs1[o - 1]
    s1[...] = total
    second = []
    for o in range(1, n_tm):
        peer = line[o - 1]
        second.append(send(s1.at[peer[1]], rs2.at[o - 1], sem_b, o - 1, peer))

    total = part_r[me_t]
    for o in range(1, n_tm):
        rhs_first[o - 1].wait_recv()
        total = total + rhs_in[o - 1]
    rhs_all[me_s] = total
    rhs_second = []
    for o in range(1, n_src):
        rhs_second.append(send(rhs_all.at[me_s], rhs_all.at[me_s], sem_q, o - 1, side[o - 1]))
    total = s1[me_t]
    for o in range(1, n_tm):
        second[o - 1].wait_recv()
        total = total + rs2[o - 1]
    full[own_rows] = total
    third = []
    for o in range(1, n_src):
        third.append(send(full.at[own_rows], full.at[own_rows], sem_c, o - 1, side[o - 1]))
    for copy in first + second + rhs_first:
        copy.wait_send()
    for copy in rhs_second:
        copy.wait()
    rhs = rhs_all[0]
    for s in range(1, n_src):
        rhs = rhs + rhs_all[s]
    for copy in third:
        copy.wait()

    whole = jnp.concatenate([rhs, full[0:40]], 0)
    stage[0] = whole[:, 0, :]
    stage[1] = whole[:, 7, :]
    to_behind = send(stage.at[0], halo.at[0], sem_d, 0, line[n_tm - 2])
    to_ahead = send(stage.at[1], halo.at[1], sem_d, 1, line[0])
    ext[:, 0:8, :] = whole
    ext[:, 8:16, :] = jnp.zeros((44, 8, 128), jnp.float32)
    to_behind.wait()
    to_ahead.wait()
    ext[:, 8, :] = halo[0] * jnp.where(me_t < n_tm - 1, 1.0, 0.0)
    ext[:, 15, :] = halo[1] * jnp.where(me_t > 0, 1.0, 0.0)

    row = lax.broadcasted_iota(jnp.int32, (1, 16, 128), 1)
    kept = jnp.where(row < 8, 1.0, 0.0)
    kept = kept + jnp.where(row == 8, 1.0, 0.0) * jnp.where(me_t < n_tm - 1, 1.0, 0.0)
    kept = kept + jnp.where(row == 15, 1.0, 0.0) * jnp.where(me_t > 0, 1.0, 0.0)
    columns = []
    for d in range(4):
        for e in range(4):
            columns.append(
                jnp.stack(
                    [
                        ext[4 + 10 * d + component_pairs.index((min(c, e), max(c, e)))]
                        for c in range(4)
                    ],
                    0,
                )
            )

    def multiply(d, x):
        value = columns[4 * d] * x[0:1]
        for e in range(1, 4):
            value = value + columns[4 * d + e] * x[e : e + 1]
        return value

    def image_of(x):
        value = prior_attitude * x + multiply(0, x)
        for d in range(1, 4):
            value = value + multiply(d, shifted(x, d)) + shifted(multiply(d, x), -d)
        return value * kept

    resid = ext[0:4]
    direction = resid
    field = None
    image = None
    alpha = None
    gamma_old = None
    for step in range(ITERS):
        applied = image_of(resid)
        inner = resid[:, 0:8, :]
        red[step, 0] = jnp.sum(inner * inner, axis=0)
        red[step, 1] = jnp.sum(inner * applied[:, 0:8, :], axis=0)
        sums = []
        for o in range(1, n_tm):
            sums.append(
                send(red.at[step], red_in.at[step, o - 1], sem_e, step * (n_tm - 1) + o - 1, line[o - 1])
            )
        value = red[step]
        for o in range(1, n_tm):
            sums[o - 1].wait()
            value = value + red_in[step, o - 1]
        gamma = jnp.sum(value[0:1], axis=(1, 2), keepdims=True)
        delta = jnp.sum(value[1:2], axis=(1, 2), keepdims=True)
        if step == 0:
            alpha = gamma / delta
            direction, image = resid, applied
            field = alpha * direction
        else:
            beta = gamma / gamma_old
            alpha = gamma / (delta - beta * (gamma / alpha))
            direction = resid + beta * direction
            image = applied + beta * image
            field = field + alpha * direction
        resid = resid - alpha * image
        gamma_old = gamma
    for k in range(8):
        out_ref[:, 128 * k : 128 * k + 128] = field[:, k, :]


def body(
    n_src,
    n_tm,
    attitude_design,
    source_design,
    scan_phase,
    obs_weight,
    obs_residual,
    source_id,
    knot_start,
    time_segment,
):
    n_obs = scan_phase.shape[0]
    f32, bf16 = jnp.float32, jnp.bfloat16
    flat = lambda x: x.reshape(1, n_obs)
    rows_all = -(-40 // n_src) * n_src
    rows = rows_all // n_src
    part_s = SRC_GROUPS // n_tm
    sems = lambda count: pltpu.SemaphoreType.DMA((2, count))
    update, field = pl.pallas_call(
        functools.partial(kernel, n_src, n_tm),
        out_shape=[jax.ShapeDtypeStruct((5, S_DEV), f32), jax.ShapeDtypeStruct((4, KS), f32)],
        in_specs=[pl.BlockSpec(memory_space=pltpu.VMEM)] * 8,
        out_specs=[pl.BlockSpec(memory_space=pltpu.VMEM)] * 2,
        scratch_shapes=[
            pltpu.VMEM((SRC_GROUPS, 24, SRC_WIDE), f32),
            pltpu.VMEM((n_tm - 1, part_s, 24, SRC_WIDE), f32),
            pltpu.VMEM((SRC_GROUPS, 8, SRC_WIDE), f32),
            pltpu.VMEM((48 * SRC_GROUPS, n_obs), bf16),
            pltpu.VMEM((2 * FEATS, n_obs), f32),
            pltpu.VMEM((2 * FEATS * n_tm, n_obs), bf16),
            pltpu.VMEM((2 * FEATS * n_tm, KS), f32),
            pltpu.VMEM((32, n_obs), f32),
            pltpu.VMEM((32 * n_tm, n_obs), bf16),
            pltpu.VMEM((32 * n_tm, KS), f32),
            pltpu.VMEM((n_tm, rows_all, 8, 128), f32),
            pltpu.VMEM((n_tm, 4, 8, 128), f32),
            pltpu.VMEM((n_src - 1, n_tm, rows, 8, 128), f32),
            pltpu.VMEM((n_tm, rows, 8, 128), f32),
            pltpu.VMEM((n_tm - 1, rows, 8, 128), f32),
            pltpu.VMEM((rows_all, 8, 128), f32),
            pltpu.VMEM((n_tm - 1, 4, 8, 128), f32),
            pltpu.VMEM((n_src, 4, 8, 128), f32),
            pltpu.VMEM((2, 44, 128), f32),
            pltpu.VMEM((2, 44, 128), f32),
            pltpu.VMEM((44, 16, 128), f32),
            pltpu.VMEM((ITERS, 2, 8, 128), f32),
            pltpu.VMEM((ITERS, n_tm - 1, 2, 8, 128), f32),
            sems(n_tm - 1),
            sems(n_tm - 1),
            sems(n_src - 1),
            sems(n_tm - 1),
            sems(n_src - 1),
            sems(n_tm - 1),
            sems(n_src - 1),
            sems(2),
            sems(ITERS * (n_tm - 1)),
        ],
        compiler_params=pltpu.CompilerParams(
            collective_id=0, has_side_effects=True, vmem_limit_bytes=56 * 1024 * 1024
        ),
    )(
        attitude_design,
        source_design,
        flat(scan_phase),
        flat(obs_weight),
        flat(obs_residual),
        flat(source_id),
        flat(knot_start),
        flat(time_segment),
    )
    return update, field


def solution(mesh):
    n_src, n_tm = mesh.shape["src"], mesh.shape["tm"]
    both = ("src", "tm")
    in_specs = (
        P(None, both),
        P(None, both),
        P(both),
        P(both),
        P(both),
        P(both),
        P(both),
        P(both, None),
    )
    out_specs = (P(None, "src"), P(None, "tm"))
    return jax.shard_map(
        functools.partial(body, n_src, n_tm),
        mesh=mesh,
        in_specs=in_specs,
        out_specs=out_specs,
        check_vma=False,
    )
```

```python
import functools

import jax
import jax.numpy as jnp
from jax import lax
from jax.experimental import pallas as pl
from jax.experimental.pallas import tpu as pltpu
from jax.sharding import PartitionSpec as P

KS = 1024
S_DEV = 2048
ITERS = 4
ROOMS = (40, 32, 24, 16)
FEATS = sum(ROOMS)
SRC_GROUPS = 8
SRC_WIDE = S_DEV // SRC_GROUPS
MESH = pl.DeviceIdType.MESH

prior_source = 1.0
prior_attitude = 1.0
index_pairs = [(i, j) for i in range(5) for j in range(i, 5)]
component_pairs = [(c, e) for c in range(4) for e in range(c, 4)]
NT = (((1,), (1,)), ((), ()))


def split(x):
    high = x.astype(jnp.bfloat16)
    low = (x - high.astype(jnp.float32)).astype(jnp.bfloat16)
    return high, low


def onehot(count, index, base):
    place = lax.broadcasted_iota(jnp.int32, (count, index.shape[1]), 0) + base
    return jnp.where(place == index, 1.0, 0.0).astype(jnp.bfloat16)


def solve_five(normals):
    entry = {}
    for n, (i, j) in enumerate(index_pairs):
        entry[j, i] = normals[n]
    for i in range(5):
        entry[i, i] = entry[i, i] + prior_source
    lower = {}
    for i in range(5):
        for j in range(i + 1):
            value = entry[i, j]
            for k in range(j):
                value = value - lower[i, k] * lower[j, k]
            if i == j:
                lower[i, i] = jnp.sqrt(value)
            else:
                lower[i, j] = value / lower[j, j]
    forward = []
    for i in range(5):
        value = normals[15 + i]
        for k in range(i):
            value = value - lower[i, k] * forward[k]
        forward.append(value / lower[i, i])
    result = [None] * 5
    for i in range(4, -1, -1):
        value = forward[i]
        for k in range(i + 1, 5):
            value = value - lower[k, i] * result[k]
        result[i] = value / lower[i, i]
    return result


def send(src, dst, sems, slot, peer):
    copy = pltpu.make_async_remote_copy(
        src_ref=src,
        dst_ref=dst,
        send_sem=sems.at[0, slot],
        recv_sem=sems.at[1, slot],
        device_id=peer,
        device_id_type=MESH,
    )
    copy.start()
    return copy


def shifted(x, by):
    lane = lax.broadcasted_iota(jnp.int32, x.shape, 2)
    turned = pltpu.roll(x, (128 - by) % 128, 2)
    if by > 0:
        return jnp.where(lane >= 128 - by, pltpu.roll(turned, x.shape[1] - 1, 1), turned)
    return jnp.where(lane < -by, pltpu.roll(turned, 1, 1), turned)


def source_sums(design, w, r, ids, lhs, own_ref):
    q = [design[i : i + 1, :] for i in range(5)]
    wq = [w * q[i] for i in range(5)]
    rows = [wq[i] * q[j] for i, j in index_pairs] + [wq[i] * r for i in range(5)]
    rows += [jnp.zeros_like(w)] * 4
    high, low = split(jnp.concatenate(rows, 0))
    both = jnp.concatenate([high.astype(jnp.float32), low.astype(jnp.float32)], 0)
    group = ids // SRC_WIDE
    for a in range(SRC_GROUPS):
        lhs[48 * a : 48 * a + 48, :] = jnp.where(group == a, both, 0.0).astype(jnp.bfloat16)
    hot = onehot(SRC_WIDE, ids % SRC_WIDE, 0)
    got = lax.dot_general(lhs[...], hot, NT, preferred_element_type=jnp.float32)
    for a in range(SRC_GROUPS):
        own_ref[a] = got[48 * a : 48 * a + 24] + got[48 * a + 24 : 48 * a + 48]


def behind(value, by, carried, lane):
    value = pltpu.roll(value, by, 1)
    front = 0.0 if carried is None else carried
    return value, jnp.where(lane < by, front, value)


def kernel(
    n_src, n_tm,
    attitude_ref, design_ref, phase_ref, weight_ref, resid_ref, id_ref, start_ref, segment_ref,
    update_ref, out_ref,
    own, landed, gathered, lhs_s, feat, lhs, acc, feat_r, lhs_r, acc_r,
    part, part_r, rs1, s1, rs2, segs, full, rhs_in, rhs_all, rhs_full, found,
    sem_n, sem_g, sem_a, sem_b, sem_c, sem_p, sem_q, sem_d, sem_e,
):
    me_s, me_t = lax.axis_index("src"), lax.axis_index("tm")
    n_obs = phase_ref.shape[1]
    side = [(lax.rem(me_s + o, n_src), me_t) for o in range(1, n_src)]
    line = [(me_s, lax.rem(me_t + o, n_tm)) for o in range(1, n_tm)]
    barrier = pltpu.get_barrier_semaphore()
    for peer in side + line:
        pl.semaphore_signal(barrier, inc=1, device_id=peer, device_id_type=MESH)

    w, ids = weight_ref[...], id_ref[...]
    source_sums(design_ref, w, resid_ref[...], ids, lhs_s, own)
    pl.semaphore_wait(barrier, len(side) + len(line))
    part_s = SRC_GROUPS // n_tm
    normals = []
    for o in range(1, n_tm):
        peer = line[o - 1]
        normals.append(
            send(own.at[pl.ds(peer[1] * part_s, part_s)], landed.at[o - 1], sem_n, o - 1, peer)
        )

    t = phase_ref[...]
    rest = 1.0 - t
    square = t * t
    cube = square * t
    basis = [
        rest * rest * rest / 6.0,
        (3.0 * cube - 6.0 * square + 4.0) / 6.0,
        (-3.0 * cube + 3.0 * square + 3.0 * t + 1.0) / 6.0,
        cube / 6.0,
    ]
    att = attitude_ref[...]
    outer = jnp.concatenate([att[c : c + 1] * att[e : e + 1] for c, e in component_pairs], 0)
    top = 0
    for j in range(4):
        scaled = w * basis[j]
        pieces = [outer * (scaled * basis[j + d]) for d in range(4 - j)]
        if ROOMS[j] > 40 - 10 * j:
            pieces.append(jnp.zeros((ROOMS[j] - 40 + 10 * j, n_obs), jnp.float32))
        high, low = split(jnp.concatenate(pieces, 0))
        feat[top : top + ROOMS[j], :] = high.astype(jnp.float32)
        feat[FEATS + top : FEATS + top + ROOMS[j], :] = low.astype(jnp.float32)
        top += ROOMS[j]
    segment, start = segment_ref[...], start_ref[...]
    tall = 2 * FEATS
    for s in range(n_tm):
        lhs[tall * s : tall * s + tall, :] = jnp.where(segment == s, feat[...], 0.0).astype(
            jnp.bfloat16
        )

    def tile(n, carry):
        knots = onehot(256, start, n * 256)
        place = pl.ds(pl.multiple_of(n * 256, 256), 256)
        acc[:, place] = lax.dot_general(lhs[...], knots, NT, preferred_element_type=jnp.float32)
        return carry

    tiles = KS // 256
    lax.fori_loop(0, tiles // 2, tile, 0)

    mine = pl.ds(me_t * part_s, part_s)
    total = own[mine]
    for o in range(1, n_tm):
        normals[o - 1].wait_recv()
        total = total + landed[o - 1]
    solved = solve_five([total[:, n, :] for n in range(20)])
    for g in range(part_s):
        for i in range(5):
            gathered[me_t * part_s + g, i : i + 1, :] = solved[i][g : g + 1, :]
        gathered[me_t * part_s + g, 5:8, :] = jnp.zeros((3, SRC_WIDE), jnp.float32)
    gathers = []
    for o in range(1, n_tm):
        gathers.append(send(gathered.at[mine], gathered.at[mine], sem_g, o - 1, line[o - 1]))

    lax.fori_loop(tiles // 2, tiles, tile, 0)

    lane = lax.broadcasted_iota(jnp.int32, (1, KS), 1)
    rows_all = part.shape[1]
    before = [None] * 4
    for s in range(n_tm):
        total = None
        top = tall * s
        for j in range(4):
            room, size = ROOMS[j], 40 - 10 * j
            value = acc[top : top + room, :] + acc[FEATS + top : FEATS + top + room, :]
            top += room
            if j == 0:
                total = value
                continue
            before[j], value = behind(value, j, before[j], lane)
            total = total + jnp.concatenate([value, jnp.zeros((40 - room, KS), jnp.float32)], 0)
        part[s, 0:40] = total.reshape(40, 8, 128)
        if rows_all > 40:
            part[s, 40:rows_all] = jnp.zeros((rows_all - 40, 8, 128), jnp.float32)
    rows = rows_all // n_src
    first = []
    for o in range(1, n_src):
        peer = side[o - 1]
        first.append(
            send(part.at[:, pl.ds(peer[0] * rows, rows)], rs1.at[o - 1], sem_a, o - 1, peer)
        )

    for copy in gathers:
        copy.wait()
    for copy in normals:
        copy.wait_send()
    for a in range(SRC_GROUPS):
        update_ref[:, a * SRC_WIDE : (a + 1) * SRC_WIDE] = gathered[a, 0:5]
    group = ids // SRC_WIDE
    hot = onehot(SRC_WIDE, ids % SRC_WIDE, 0)
    high, low = split(gathered[...].reshape(SRC_GROUPS * 8, SRC_WIDE))
    picks = jnp.dot(high, hot, preferred_element_type=jnp.float32) + jnp.dot(
        low, hot, preferred_element_type=jnp.float32
    )
    picked = jnp.zeros((8, n_obs), jnp.float32)
    for a in range(SRC_GROUPS):
        picked = picked + jnp.where(group == a, picks[8 * a : 8 * a + 8], 0.0)
    fitted = jnp.sum(design_ref[...] * picked[0:5], axis=0, keepdims=True)
    weighted = w * (resid_ref[...] - fitted)
    high, low = split(jnp.concatenate([att * (weighted * basis[j]) for j in range(4)], 0))
    feat_r[0:16, :] = high.astype(jnp.float32)
    feat_r[16:32, :] = low.astype(jnp.float32)
    for s in range(n_tm):
        lhs_r[32 * s : 32 * s + 32, :] = jnp.where(segment == s, feat_r[...], 0.0).astype(
            jnp.bfloat16
        )

    def tile_r(n, carry):
        knots = onehot(256, start, n * 256)
        place = pl.ds(pl.multiple_of(n * 256, 256), 256)
        acc_r[:, place] = lax.dot_general(lhs_r[...], knots, NT, preferred_element_type=jnp.float32)
        return carry

    lax.fori_loop(0, tiles // 2, tile_r, 0)
    own_rows = pl.ds(me_s * rows, rows)
    total = part[:, own_rows]
    for o in range(1, n_src):
        first[o - 1].wait_recv()
        total = total + rs1[o - 1]
    s1[...] = total
    second = []
    for o in range(1, n_tm):
        peer = line[o - 1]
        second.append(send(s1.at[peer[1]], rs2.at[o - 1], sem_b, o - 1, peer))
    lax.fori_loop(tiles // 2, tiles, tile_r, 0)
    before = [None] * 4
    for s in range(n_tm):
        total = None
        for j in range(4):
            top = 32 * s + 4 * j
            value = acc_r[top : top + 4, :] + acc_r[16 + top : 20 + top, :]
            if j == 0:
                total = value
                continue
            before[j], value = behind(value, j, before[j], lane)
            total = total + value
        part_r[s] = total.reshape(4, 8, 128)

    rhs_first = []
    for o in range(1, n_tm):
        peer = line[o - 1]
        rhs_first.append(send(part_r.at[peer[1]], rhs_in.at[o - 1], sem_p, o - 1, peer))
    total = s1[me_t]
    for o in range(1, n_tm):
        second[o - 1].wait_recv()
        total = total + rs2[o - 1]
    segs[me_t] = total
    spread = []
    for o in range(1, n_tm):
        spread.append(send(segs.at[me_t], segs.at[me_t], sem_d, o - 1, line[o - 1]))

    total = part_r[me_t]
    for o in range(1, n_tm):
        rhs_first[o - 1].wait_recv()
        total = total + rhs_in[o - 1]
    rhs_all[me_s] = total
    rhs_second = []
    for o in range(1, n_src):
        rhs_second.append(send(rhs_all.at[me_s], rhs_all.at[me_s], sem_q, o - 1, side[o - 1]))
    for copy in spread:
        copy.wait()
    third = []
    for o in range(1, n_src):
        third.append(send(segs, full.at[me_s], sem_c, o - 1, side[o - 1]))
    full[me_s] = segs[...]
    for copy in rhs_second:
        copy.wait()
    rhs = rhs_all[0]
    for s in range(1, n_src):
        rhs = rhs + rhs_all[s]
    rhs_full[me_t] = rhs
    rhs_third = []
    for o in range(1, n_tm):
        rhs_third.append(send(rhs_full.at[me_t], rhs_full.at[me_t], sem_e, o - 1, line[o - 1]))
    for copy in first + second + rhs_first:
        copy.wait_send()
    for copy in rhs_third:
        copy.wait()
    for copy in third:
        copy.wait()

    tall = 8 * n_tm
    knot = lax.broadcasted_iota(jnp.int32, (tall, 128), 0) * 128
    knot = knot + lax.broadcasted_iota(jnp.int32, (tall, 128), 1)
    columns = []
    for d in range(4):
        bands = []
        for q in range(10):
            place = 10 * d + q
            band = full[place // rows, :, place % rows].reshape(tall, 128)
            bands.append(band if d == 0 else jnp.where(knot < tall * 128 - d, band, 0.0))
        for e in range(4):
            columns.append(
                jnp.stack(
                    [bands[component_pairs.index((min(c, e), max(c, e)))] for c in range(4)], 0
                )
            )

    def multiply(d, x):
        value = columns[4 * d] * x[0:1]
        for e in range(1, 4):
            value = value + columns[4 * d + e] * x[e : e + 1]
        return value

    def image_of(x):
        value = prior_attitude * x + multiply(0, x)
        for d in range(1, 4):
            value = value + multiply(d, shifted(x, d)) + shifted(multiply(d, x), -d)
        return value

    def inner(x, y):
        lanes = jnp.sum(x * y, axis=(0, 1), keepdims=True)
        return jnp.sum(lanes, axis=2, keepdims=True)

    resid = jnp.stack([rhs_full[:, c].reshape(tall, 128) for c in range(4)], 0)
    direction = resid
    field = jnp.zeros_like(resid)
    norm_now = inner(resid, resid)
    for step in range(ITERS):
        image = image_of(direction)
        alpha = norm_now / inner(direction, image)
        field = field + alpha * direction
        if step < ITERS - 1:
            resid = resid - alpha * image
            norm_next = inner(resid, resid)
            direction = resid + norm_next / norm_now * direction
            norm_now = norm_next
    found[...] = field.reshape(4, n_tm, 8, 128)
    mine = found[:, me_t]
    for k in range(8):
        out_ref[:, 128 * k : 128 * k + 128] = mine[:, k, :]


def body(
    n_src,
    n_tm,
    attitude_design,
    source_design,
    scan_phase,
    obs_weight,
    obs_residual,
    source_id,
    knot_start,
    time_segment,
):
    n_obs = scan_phase.shape[0]
    f32, bf16 = jnp.float32, jnp.bfloat16
    flat = lambda x: x.reshape(1, n_obs)
    rows_all = -(-40 // n_src) * n_src
    rows = rows_all // n_src
    part_s = SRC_GROUPS // n_tm
    sems = lambda count: pltpu.SemaphoreType.DMA((2, count))
    update, field = pl.pallas_call(
        functools.partial(kernel, n_src, n_tm),
        out_shape=[jax.ShapeDtypeStruct((5, S_DEV), f32), jax.ShapeDtypeStruct((4, KS), f32)],
        in_specs=[pl.BlockSpec(memory_space=pltpu.VMEM)] * 8,
        out_specs=[pl.BlockSpec(memory_space=pltpu.VMEM)] * 2,
        scratch_shapes=[
            pltpu.VMEM((SRC_GROUPS, 24, SRC_WIDE), f32),
            pltpu.VMEM((n_tm - 1, part_s, 24, SRC_WIDE), f32),
            pltpu.VMEM((SRC_GROUPS, 8, SRC_WIDE), f32),
            pltpu.VMEM((48 * SRC_GROUPS, n_obs), bf16),
            pltpu.VMEM((2 * FEATS, n_obs), f32),
            pltpu.VMEM((2 * FEATS * n_tm, n_obs), bf16),
            pltpu.VMEM((2 * FEATS * n_tm, KS), f32),
            pltpu.VMEM((32, n_obs), f32),
            pltpu.VMEM((32 * n_tm, n_obs), bf16),
            pltpu.VMEM((32 * n_tm, KS), f32),
            pltpu.VMEM((n_tm, rows_all, 8, 128), f32),
            pltpu.VMEM((n_tm, 4, 8, 128), f32),
            pltpu.VMEM((n_src - 1, n_tm, rows, 8, 128), f32),
            pltpu.VMEM((n_tm, rows, 8, 128), f32),
            pltpu.VMEM((n_tm - 1, rows, 8, 128), f32),
            pltpu.VMEM((n_tm, rows, 8, 128), f32),
            pltpu.VMEM((n_src, n_tm, rows, 8, 128), f32),
            pltpu.VMEM((n_tm - 1, 4, 8, 128), f32),
            pltpu.VMEM((n_src, 4, 8, 128), f32),
            pltpu.VMEM((n_tm, 4, 8, 128), f32),
            pltpu.VMEM((4, n_tm, 8, 128), f32),
            sems(n_tm - 1),
            sems(n_tm - 1),
            sems(n_src - 1),
            sems(n_tm - 1),
            sems(n_src - 1),
            sems(n_tm - 1),
            sems(n_src - 1),
            sems(n_tm - 1),
            sems(n_tm - 1),
        ],
        compiler_params=pltpu.CompilerParams(
            collective_id=0, has_side_effects=True, vmem_limit_bytes=56 * 1024 * 1024
        ),
    )(
        attitude_design,
        source_design,
        flat(scan_phase),
        flat(obs_weight),
        flat(obs_residual),
        flat(source_id),
        flat(knot_start),
        flat(time_segment),
    )
    return update, field


def solution(mesh):
    n_src, n_tm = mesh.shape["src"], mesh.shape["tm"]
    both = ("src", "tm")
    in_specs = (
        P(None, both),
        P(None, both),
        P(both),
        P(both),
        P(both),
        P(both),
        P(both),
        P(both, None),
    )
    out_specs = (P(None, "src"), P(None, "tm"))
    return jax.shard_map(
        functools.partial(body, n_src, n_tm),
        mesh=mesh,
        in_specs=in_specs,
        out_specs=out_specs,
        check_vma=False,
    )
```

```python
import functools

import jax
import jax.numpy as jnp
from jax import lax
from jax.experimental import pallas as pl
from jax.experimental.pallas import tpu as pltpu
from jax.sharding import PartitionSpec as P

KS = 1024
S_DEV = 2048
ITERS = 4
ROOMS = (40, 32, 24, 16)
FEATS = sum(ROOMS)
SRC_GROUPS = 8
SRC_WIDE = S_DEV // SRC_GROUPS
MESH = pl.DeviceIdType.MESH

prior_source = 1.0
prior_attitude = 1.0
index_pairs = [(i, j) for i in range(5) for j in range(i, 5)]
component_pairs = [(c, e) for c in range(4) for e in range(c, 4)]
NT = (((1,), (1,)), ((), ()))


def split(x):
    high = x.astype(jnp.bfloat16)
    low = (x - high.astype(jnp.float32)).astype(jnp.bfloat16)
    return high, low


def onehot(count, index, base):
    place = lax.broadcasted_iota(jnp.int32, (count, index.shape[1]), 0) + base
    return jnp.where(place == index, 1.0, 0.0).astype(jnp.bfloat16)


def solve_five(normals):
    entry = {}
    for n, (i, j) in enumerate(index_pairs):
        entry[j, i] = normals[n]
    for i in range(5):
        entry[i, i] = entry[i, i] + prior_source
    lower = {}
    for i in range(5):
        for j in range(i + 1):
            value = entry[i, j]
            for k in range(j):
                value = value - lower[i, k] * lower[j, k]
            if i == j:
                lower[i, i] = jnp.sqrt(value)
            else:
                lower[i, j] = value / lower[j, j]
    forward = []
    for i in range(5):
        value = normals[15 + i]
        for k in range(i):
            value = value - lower[i, k] * forward[k]
        forward.append(value / lower[i, i])
    result = [None] * 5
    for i in range(4, -1, -1):
        value = forward[i]
        for k in range(i + 1, 5):
            value = value - lower[k, i] * result[k]
        result[i] = value / lower[i, i]
    return result


def send(src, dst, sems, slot, peer):
    copy = pltpu.make_async_remote_copy(
        src_ref=src,
        dst_ref=dst,
        send_sem=sems.at[0, slot],
        recv_sem=sems.at[1, slot],
        device_id=peer,
        device_id_type=MESH,
    )
    copy.start()
    return copy


def shifted(x, by):
    lane = lax.broadcasted_iota(jnp.int32, x.shape, 2)
    turned = pltpu.roll(x, (128 - by) % 128, 2)
    if by > 0:
        return jnp.where(lane >= 128 - by, pltpu.roll(turned, x.shape[1] - 1, 1), turned)
    return jnp.where(lane < -by, pltpu.roll(turned, 1, 1), turned)


def source_sums(design, w, r, ids, lhs, own_ref):
    q = [design[i : i + 1, :] for i in range(5)]
    wq = [w * q[i] for i in range(5)]
    rows = [wq[i] * q[j] for i, j in index_pairs] + [wq[i] * r for i in range(5)]
    rows += [jnp.zeros_like(w)] * 4
    high, low = split(jnp.concatenate(rows, 0))
    both = jnp.concatenate([high.astype(jnp.float32), low.astype(jnp.float32)], 0)
    group = ids // SRC_WIDE
    for a in range(SRC_GROUPS):
        lhs[48 * a : 48 * a + 48, :] = jnp.where(group == a, both, 0.0).astype(jnp.bfloat16)
    hot = onehot(SRC_WIDE, ids % SRC_WIDE, 0)
    got = lax.dot_general(lhs[...], hot, NT, preferred_element_type=jnp.float32)
    for a in range(SRC_GROUPS):
        own_ref[a] = got[48 * a : 48 * a + 24] + got[48 * a + 24 : 48 * a + 48]


def behind(value, by, carried, lane):
    value = pltpu.roll(value, by, 1)
    front = 0.0 if carried is None else carried
    return value, jnp.where(lane < by, front, value)


def kernel(
    n_src, n_tm,
    attitude_ref, design_ref, phase_ref, weight_ref, resid_ref, id_ref, start_ref, segment_ref,
    update_ref, out_ref,
    own, landed, gathered, lhs_s, feat, lhs, acc, feat_r, lhs_r, acc_r,
    part, part_r, rs1, s1, rs2, segs, full, rhs_in, rhs_all, rhs_full, found,
    sem_n, sem_g, sem_a, sem_b, sem_c, sem_p, sem_q, sem_d, sem_e,
):
    me_s, me_t = lax.axis_index("src"), lax.axis_index("tm")
    n_obs = phase_ref.shape[1]
    side = [(lax.rem(me_s + o, n_src), me_t) for o in range(1, n_src)]
    line = [(me_s, lax.rem(me_t + o, n_tm)) for o in range(1, n_tm)]
    barrier = pltpu.get_barrier_semaphore()
    for peer in side + line:
        pl.semaphore_signal(barrier, inc=1, device_id=peer, device_id_type=MESH)

    w, ids = weight_ref[...], id_ref[...]
    source_sums(design_ref, w, resid_ref[...], ids, lhs_s, own)
    pl.semaphore_wait(barrier, len(side) + len(line))
    part_s = SRC_GROUPS // n_tm
    normals = []
    for o in range(1, n_tm):
        peer = line[o - 1]
        normals.append(
            send(own.at[pl.ds(peer[1] * part_s, part_s)], landed.at[o - 1], sem_n, o - 1, peer)
        )

    t = phase_ref[...]
    rest = 1.0 - t
    square = t * t
    cube = square * t
    basis = [
        rest * rest * rest / 6.0,
        (3.0 * cube - 6.0 * square + 4.0) / 6.0,
        (-3.0 * cube + 3.0 * square + 3.0 * t + 1.0) / 6.0,
        cube / 6.0,
    ]
    att = attitude_ref[...]
    outer = jnp.concatenate([att[c : c + 1] * att[e : e + 1] for c, e in component_pairs], 0)
    top = 0
    for j in range(4):
        scaled = w * basis[j]
        pieces = [outer * (scaled * basis[j + d]) for d in range(4 - j)]
        if ROOMS[j] > 40 - 10 * j:
            pieces.append(jnp.zeros((ROOMS[j] - 40 + 10 * j, n_obs), jnp.float32))
        high, low = split(jnp.concatenate(pieces, 0))
        feat[top : top + ROOMS[j], :] = high.astype(jnp.float32)
        feat[FEATS + top : FEATS + top + ROOMS[j], :] = low.astype(jnp.float32)
        top += ROOMS[j]
    segment, start = segment_ref[...], start_ref[...]
    tall = 2 * FEATS
    tiles = KS // 256
    half = n_tm // 2
    lane = lax.broadcasted_iota(jnp.int32, (1, KS), 1)
    rows_all = part.shape[1]
    rows = rows_all // n_src
    before = [None] * 4
    first = []

    def band_half(begin):
        for s in range(begin, begin + half):
            lhs[tall * s : tall * s + tall, :] = jnp.where(segment == s, feat[...], 0.0).astype(
                jnp.bfloat16
            )
        low_row, high_row = tall * begin, tall * (begin + half)

        def tile(n, carry):
            knots = onehot(256, start, n * 256)
            place = pl.ds(pl.multiple_of(n * 256, 256), 256)
            acc[low_row:high_row, place] = lax.dot_general(
                lhs[low_row:high_row, :], knots, NT, preferred_element_type=jnp.float32
            )
            return carry

        lax.fori_loop(0, tiles, tile, 0)
        for s in range(begin, begin + half):
            total = None
            top = tall * s
            for j in range(4):
                room = ROOMS[j]
                value = acc[top : top + room, :] + acc[FEATS + top : FEATS + top + room, :]
                top += room
                if j == 0:
                    total = value
                    continue
                before[j], value = behind(value, j, before[j], lane)
                total = total + jnp.concatenate([value, jnp.zeros((40 - room, KS), jnp.float32)], 0)
            part[s, 0:40] = total.reshape(40, 8, 128)
            if rows_all > 40:
                part[s, 40:rows_all] = jnp.zeros((rows_all - 40, 8, 128), jnp.float32)
        some = pl.ds(begin, half)
        for o in range(1, n_src):
            peer = side[o - 1]
            first.append(
                send(
                    part.at[some, pl.ds(peer[0] * rows, rows)],
                    rs1.at[o - 1, some],
                    sem_a,
                    len(first),
                    peer,
                )
            )

    band_half(0)

    mine = pl.ds(me_t * part_s, part_s)
    total = own[mine]
    for o in range(1, n_tm):
        normals[o - 1].wait_recv()
        total = total + landed[o - 1]
    solved = solve_five([total[:, n, :] for n in range(20)])
    for g in range(part_s):
        for i in range(5):
            gathered[me_t * part_s + g, i : i + 1, :] = solved[i][g : g + 1, :]
        gathered[me_t * part_s + g, 5:8, :] = jnp.zeros((3, SRC_WIDE), jnp.float32)
    gathers = []
    for o in range(1, n_tm):
        gathers.append(send(gathered.at[mine], gathered.at[mine], sem_g, o - 1, line[o - 1]))

    band_half(half)

    for copy in gathers:
        copy.wait()
    for copy in normals:
        copy.wait_send()
    for a in range(SRC_GROUPS):
        update_ref[:, a * SRC_WIDE : (a + 1) * SRC_WIDE] = gathered[a, 0:5]
    group = ids // SRC_WIDE
    hot = onehot(SRC_WIDE, ids % SRC_WIDE, 0)
    high, low = split(gathered[...].reshape(SRC_GROUPS * 8, SRC_WIDE))
    picks = jnp.dot(high, hot, preferred_element_type=jnp.float32) + jnp.dot(
        low, hot, preferred_element_type=jnp.float32
    )
    picked = jnp.zeros((8, n_obs), jnp.float32)
    for a in range(SRC_GROUPS):
        picked = picked + jnp.where(group == a, picks[8 * a : 8 * a + 8], 0.0)
    fitted = jnp.sum(design_ref[...] * picked[0:5], axis=0, keepdims=True)
    weighted = w * (resid_ref[...] - fitted)
    high, low = split(jnp.concatenate([att * (weighted * basis[j]) for j in range(4)], 0))
    feat_r[0:16, :] = high.astype(jnp.float32)
    feat_r[16:32, :] = low.astype(jnp.float32)
    for s in range(n_tm):
        lhs_r[32 * s : 32 * s + 32, :] = jnp.where(segment == s, feat_r[...], 0.0).astype(
            jnp.bfloat16
        )

    def tile_r(n, carry):
        knots = onehot(256, start, n * 256)
        place = pl.ds(pl.multiple_of(n * 256, 256), 256)
        acc_r[:, place] = lax.dot_general(lhs_r[...], knots, NT, preferred_element_type=jnp.float32)
        return carry

    lax.fori_loop(0, tiles // 2, tile_r, 0)
    own_rows = pl.ds(me_s * rows, rows)
    total = part[:, own_rows]
    for o in range(1, n_src):
        first[o - 1].wait_recv()
        first[n_src - 1 + o - 1].wait_recv()
        total = total + rs1[o - 1]
    s1[...] = total
    second = []
    for o in range(1, n_tm):
        peer = line[o - 1]
        second.append(send(s1.at[peer[1]], rs2.at[o - 1], sem_b, o - 1, peer))
    lax.fori_loop(tiles // 2, tiles, tile_r, 0)
    before = [None] * 4
    for s in range(n_tm):
        total = None
        for j in range(4):
            top = 32 * s + 4 * j
            value = acc_r[top : top + 4, :] + acc_r[16 + top : 20 + top, :]
            if j == 0:
                total = value
                continue
            before[j], value = behind(value, j, before[j], lane)
            total = total + value
        part_r[s] = total.reshape(4, 8, 128)

    rhs_first = []
    for o in range(1, n_tm):
        peer = line[o - 1]
        rhs_first.append(send(part_r.at[peer[1]], rhs_in.at[o - 1], sem_p, o - 1, peer))
    total = s1[me_t]
    for o in range(1, n_tm):
        second[o - 1].wait_recv()
        total = total + rs2[o - 1]
    segs[me_t] = total
    third = []

    def pass_on(slot):
        for peer in side:
            third.append(send(segs.at[slot], full.at[me_s, slot], sem_c, len(third), peer))

    spread = []
    for o in range(1, n_tm):
        spread.append(send(segs.at[me_t], segs.at[me_t], sem_d, o - 1, line[o - 1]))

    pass_on(me_t)
    total = part_r[me_t]
    for o in range(1, n_tm):
        rhs_first[o - 1].wait_recv()
        total = total + rhs_in[o - 1]
    rhs_all[me_s] = total
    rhs_second = []
    for o in range(1, n_src):
        rhs_second.append(send(rhs_all.at[me_s], rhs_all.at[me_s], sem_q, o - 1, side[o - 1]))
    for o in range(1, n_tm):
        spread[o - 1].wait_recv()
        pass_on(lax.rem(me_t + n_tm - o, n_tm))
    full[me_s] = segs[...]
    for copy in rhs_second:
        copy.wait()
    rhs = rhs_all[0]
    for s in range(1, n_src):
        rhs = rhs + rhs_all[s]
    rhs_full[me_t] = rhs
    rhs_third = []
    for o in range(1, n_tm):
        rhs_third.append(send(rhs_full.at[me_t], rhs_full.at[me_t], sem_e, o - 1, line[o - 1]))
    for copy in first + second + rhs_first + spread:
        copy.wait_send()
    for copy in rhs_third:
        copy.wait()
    for copy in third:
        copy.wait()

    tall = 8 * n_tm
    knot = lax.broadcasted_iota(jnp.int32, (tall, 128), 0) * 128
    knot = knot + lax.broadcasted_iota(jnp.int32, (tall, 128), 1)
    columns = []
    for d in range(4):
        bands = []
        for q in range(10):
            place = 10 * d + q
            band = full[place // rows, :, place % rows].reshape(tall, 128)
            bands.append(band if d == 0 else jnp.where(knot < tall * 128 - d, band, 0.0))
        for e in range(4):
            columns.append(
                jnp.stack(
                    [bands[component_pairs.index((min(c, e), max(c, e)))] for c in range(4)], 0
                )
            )

    def multiply(d, x):
        value = columns[4 * d] * x[0:1]
        for e in range(1, 4):
            value = value + columns[4 * d + e] * x[e : e + 1]
        return value

    def image_of(x):
        value = prior_attitude * x + multiply(0, x)
        for d in range(1, 4):
            value = value + multiply(d, shifted(x, d)) + shifted(multiply(d, x), -d)
        return value

    def inner(x, y):
        lanes = jnp.sum(x * y, axis=(0, 1), keepdims=True)
        return jnp.sum(lanes, axis=2, keepdims=True)

    resid = jnp.stack([rhs_full[:, c].reshape(tall, 128) for c in range(4)], 0)
    direction = resid
    field = jnp.zeros_like(resid)
    norm_now = inner(resid, resid)
    for step in range(ITERS):
        image = image_of(direction)
        alpha = norm_now / inner(direction, image)
        field = field + alpha * direction
        if step < ITERS - 1:
            resid = resid - alpha * image
            norm_next = inner(resid, resid)
            direction = resid + norm_next / norm_now * direction
            norm_now = norm_next
    found[...] = field.reshape(4, n_tm, 8, 128)
    mine = found[:, me_t]
    for k in range(8):
        out_ref[:, 128 * k : 128 * k + 128] = mine[:, k, :]


def body(
    n_src,
    n_tm,
    attitude_design,
    source_design,
    scan_phase,
    obs_weight,
    obs_residual,
    source_id,
    knot_start,
    time_segment,
):
    n_obs = scan_phase.shape[0]
    f32, bf16 = jnp.float32, jnp.bfloat16
    flat = lambda x: x.reshape(1, n_obs)
    rows_all = -(-40 // n_src) * n_src
    rows = rows_all // n_src
    part_s = SRC_GROUPS // n_tm
    sems = lambda count: pltpu.SemaphoreType.DMA((2, count))
    update, field = pl.pallas_call(
        functools.partial(kernel, n_src, n_tm),
        out_shape=[jax.ShapeDtypeStruct((5, S_DEV), f32), jax.ShapeDtypeStruct((4, KS), f32)],
        in_specs=[pl.BlockSpec(memory_space=pltpu.VMEM)] * 8,
        out_specs=[pl.BlockSpec(memory_space=pltpu.VMEM)] * 2,
        scratch_shapes=[
            pltpu.VMEM((SRC_GROUPS, 24, SRC_WIDE), f32),
            pltpu.VMEM((n_tm - 1, part_s, 24, SRC_WIDE), f32),
            pltpu.VMEM((SRC_GROUPS, 8, SRC_WIDE), f32),
            pltpu.VMEM((48 * SRC_GROUPS, n_obs), bf16),
            pltpu.VMEM((2 * FEATS, n_obs), f32),
            pltpu.VMEM((2 * FEATS * n_tm, n_obs), bf16),
            pltpu.VMEM((2 * FEATS * n_tm, KS), f32),
            pltpu.VMEM((32, n_obs), f32),
            pltpu.VMEM((32 * n_tm, n_obs), bf16),
            pltpu.VMEM((32 * n_tm, KS), f32),
            pltpu.VMEM((n_tm, rows_all, 8, 128), f32),
            pltpu.VMEM((n_tm, 4, 8, 128), f32),
            pltpu.VMEM((n_src - 1, n_tm, rows, 8, 128), f32),
            pltpu.VMEM((n_tm, rows, 8, 128), f32),
            pltpu.VMEM((n_tm - 1, rows, 8, 128), f32),
            pltpu.VMEM((n_tm, rows, 8, 128), f32),
            pltpu.VMEM((n_src, n_tm, rows, 8, 128), f32),
            pltpu.VMEM((n_tm - 1, 4, 8, 128), f32),
            pltpu.VMEM((n_src, 4, 8, 128), f32),
            pltpu.VMEM((n_tm, 4, 8, 128), f32),
            pltpu.VMEM((4, n_tm, 8, 128), f32),
            sems(n_tm - 1),
            sems(n_tm - 1),
            sems(2 * (n_src - 1)),
            sems(n_tm - 1),
            sems(n_tm * (n_src - 1)),
            sems(n_tm - 1),
            sems(n_src - 1),
            sems(n_tm - 1),
            sems(n_tm - 1),
        ],
        compiler_params=pltpu.CompilerParams(
            collective_id=0, has_side_effects=True, vmem_limit_bytes=56 * 1024 * 1024
        ),
    )(
        attitude_design,
        source_design,
        flat(scan_phase),
        flat(obs_weight),
        flat(obs_residual),
        flat(source_id),
        flat(knot_start),
        flat(time_segment),
    )
    return update, field


def solution(mesh):
    n_src, n_tm = mesh.shape["src"], mesh.shape["tm"]
    both = ("src", "tm")
    in_specs = (
        P(None, both),
        P(None, both),
        P(both),
        P(both),
        P(both),
        P(both),
        P(both),
        P(both, None),
    )
    out_specs = (P(None, "src"), P(None, "tm"))
    return jax.shard_map(
        functools.partial(body, n_src, n_tm),
        mesh=mesh,
        in_specs=in_specs,
        out_specs=out_specs,
        check_vma=False,
    )
```
